32 devices in a mesh: grp: 2 (over x), dev: 16 (over z, y, core).
Axes of the slice: x: 2, y: 2, z: 4, core: 2. Of those that a mesh axis runs over, the one named last changes fastest.
Arguments:
- residual: bfloat16 [64, 8192], P(('grp', 'dev')), parts along dimension 0, may hold values from -8 to 8
- query: bfloat16 [64, 8192], P(('grp', 'dev')), parts along dimension 0, may hold values from -32 to 32
- latest_key_value: bfloat16 [64, 1024], P(('grp', 'dev')), parts along dimension 0, may hold values from -4 to 4
- kv_cache: bfloat16 [128, 256, 1024], P(('grp', 'dev')), parts along dimension 0, may hold values from -4 to 4
- lengths: int32 [128], P(('grp', 'dev')), parts along dimension 0, may hold values from 2 to 256, as said below
- owner_map: int32 [64], P('grp'), parts along dimension 0, may hold values from 0 to 63, as said below
- norm_gain: bfloat16 [8192], replicated, may hold values from 0.099609375 to 1.8984375
- gate_codes: float32 [512, 3, 32768], P(None, None, 'dev'), may hold values from 0 to 16777215, as said below
- gate_scale: bfloat16 [64, 32768], P(None, 'dev'), may hold values from 0.0010986328 to 0.0043945312
- gate_zero: bfloat16 [64, 32768], P(None, 'dev'), may hold values from 6 to 9
- up_codes: float32 [512, 3, 32768], P(None, None, 'dev'), may hold values from 0 to 16777215, as said below
- up_scale: bfloat16 [64, 32768], P(None, 'dev'), may hold values from 0.0010986328 to 0.0043945312
- up_zero: bfloat16 [64, 32768], P(None, 'dev'), may hold values from 6 to 9
- down_codes: float32 [2048, 3, 8192], P('dev'), may hold values from 0 to 16777215, as said below
- down_scale: bfloat16 [256, 8192], P('dev'), may hold values from 0.0005493164 to 0.0021972656
- down_zero: bfloat16 [256, 8192], P('dev'), may hold values from 6 to 9
Outputs:
- layer_output: bfloat16 [64, 8192], P(('grp', 'dev')), parts along dimension 0
The draws below stay inside these ranges and needn't reach their ends.
There are 2 independent parts, one for each index of `grp`. The reference program is written for one: setup_inputs(seed, part) draws one part's arguments, and reference() takes and returns one part's arrays. A program takes and returns all parts, laid end to end along the dimension named above; an argument that names none is the same for every part. Nothing has to cross between parts.
Inputs may be any that keep to these rules, and one draw needn't show every extreme that they name: Batch row r is served by request slot owner_map[r], numbered device * 4 + slot along dev. The values are distinct, so a device serves at most 4 rows, and in every draw some device serves exactly 4; slots that no row names are empty. `lengths`: only slots named by owner_map are read; in every draw some served slot holds exactly 256 tokens. `gate_codes`: every word is a whole number; its base-16 digits are the codes, six in words p = 0 and 1, four in word p = 2. `up_codes`: packed as gate_codes. `down_codes`: packed as gate_codes, rows being hidden units.
All inputs are finite; a program needn't handle non-finite values.
Results may differ from the reference program's by a relative error of at most 0.015.
Values may be sent and summed in bfloat16 or wider, within the bound.
A program may use at most 640 MiB of HBM per device.

```python
import math
import jax
import jax.numpy as jnp
from jax import lax

D = 8192
QUERY_HEADS = 64
KEY_VALUE_HEADS = 4
HEAD_SIZE = 128
FF = 32768
GROUP = 128
SLOTS = 4
CONTEXT_TOKENS = 256
BATCH_ROWS = 32
REQUEST_SLOTS = 64
N_DEV = 16


def owner_slots(key):
    random_subkey = jax.random.fold_in(key, 11)
    pick_key, order_key, row_key = jax.random.split(random_subkey, 3)
    full_device = jax.random.randint(pick_key, (), 0, REQUEST_SLOTS // SLOTS)
    ranking = jax.random.permutation(order_key, REQUEST_SLOTS).astype(jnp.int32)
    slot_ids = jnp.arange(REQUEST_SLOTS, dtype=jnp.int32)
    int_scores = jnp.where(slot_ids // SLOTS == full_device, slot_ids % SLOTS - SLOTS, ranking)
    chosen = jnp.argsort(int_scores)[:BATCH_ROWS]
    return chosen[jax.random.permutation(row_key, BATCH_ROWS)].astype(jnp.int32)


def packed_words(random_subkey, row_words, columns):
    words = []
    for word_slot in range(3):
        digits = 6 if word_slot < 2 else 4
        total = jnp.zeros((row_words, columns), jnp.float32)
        for place in range(digits):
            nibbles = jax.random.randint(jax.random.fold_in(random_subkey, word_slot * 8 + place), (row_words, columns), 0, 16).astype(jnp.float32)
            total = total + nibbles * 16.0 ** place
        words.append(total)
    return jnp.stack(words, axis=1)


def draw_owner_map(key, part):
    return owner_slots(key)


def draw_lengths(key, part):
    served = owner_slots(key)
    random_subkey = jax.random.fold_in(key, 2)
    span_key, length_key = jax.random.split(random_subkey)
    spans = jax.random.randint(span_key, (REQUEST_SLOTS,), 1, CONTEXT_TOKENS - 1)
    drawn = 2 + jax.random.randint(length_key, (REQUEST_SLOTS,), 0, spans)
    return drawn.at[served[0]].set(CONTEXT_TOKENS).astype(jnp.int32)


def draw_query(key, part):
    random_subkey = jax.random.fold_in(key, 3)
    return jnp.clip(jax.random.normal(random_subkey, (BATCH_ROWS, QUERY_HEADS * HEAD_SIZE), jnp.float32), -4.0, 4.0).astype(jnp.bfloat16)


def draw_kv_cache(key, part):
    random_subkey = jax.random.fold_in(key, 4)
    return jnp.clip(jax.random.normal(random_subkey, (REQUEST_SLOTS, CONTEXT_TOKENS, 2 * KEY_VALUE_HEADS * HEAD_SIZE), jnp.float32), -4.0, 4.0).astype(jnp.bfloat16)


def draw_residual(key, part):
    random_subkey = jax.random.fold_in(key, 5)
    base_key, row_key, col_key = jax.random.split(random_subkey, 3)
    row_scales = jnp.exp(jax.random.uniform(row_key, (BATCH_ROWS, 1), jnp.float32, math.log(0.2), math.log(2.0)))
    col_scales = jnp.exp(jax.random.uniform(col_key, (1, D), jnp.float32, math.log(0.1), math.log(1.0)))
    base_offset = jnp.clip(jax.random.normal(base_key, (BATCH_ROWS, D), jnp.float32), -4.0, 4.0)
    return (base_offset * row_scales * col_scales).astype(jnp.bfloat16)


def draw_gate_codes(key, part):
    random_subkey = jax.random.fold_in(key, 6)
    return packed_words(random_subkey, D // 16, FF)


def draw_up_codes(key, part):
    random_subkey = jax.random.fold_in(key, 7)
    return packed_words(random_subkey, D // 16, FF)


def draw_down_codes(key, part):
    random_subkey = jax.random.fold_in(key, 8)
    return packed_words(random_subkey, FF // 16, D)


def level_of(key, dims, cuts, least, high):
    gain = 1.0
    for position, parts in cuts:
        draws = jax.random.uniform(jax.random.fold_in(jax.random.fold_in(key, 6), position), (parts,), jnp.float32, least / len(cuts), high / len(cuts))
        gain = gain * jnp.repeat(jnp.exp(draws), dims[position] // parts).reshape((-1,) + (1,) * (len(dims) - 1 - position))
    return gain


def scatter_about(key, extent, width, reach, cuts=(), kind=jnp.bfloat16):
    entries = width * jax.random.normal(key, extent, jnp.float32)
    if cuts:
        entries = entries * level_of(key, extent, cuts, -0.22, 0.18)
    return jnp.clip(entries, -reach, reach).astype(kind)


def setup_inputs(seed: int = 0, part: int = 0) -> dict:
    splits = jax.random.split(jax.random.key(seed), 17)
    own_keys = jax.random.split(jax.random.fold_in(splits[16], part), 17)
    residual = draw_residual(jax.random.fold_in(jax.random.fold_in(splits[16], part), 71), part)
    query = draw_query(jax.random.fold_in(jax.random.fold_in(splits[16], part), 71), part)
    latest_key_value = scatter_about(own_keys[2], (BATCH_ROWS, 2 * KEY_VALUE_HEADS * HEAD_SIZE), 1.0, 4.0, ((0, 16),))
    kv_cache = draw_kv_cache(jax.random.fold_in(jax.random.fold_in(splits[16], part), 71), part)
    lengths = draw_lengths(jax.random.fold_in(jax.random.fold_in(splits[16], part), 71), part)
    owner_map = draw_owner_map(jax.random.fold_in(jax.random.fold_in(splits[16], part), 71), part)
    norm_gain = jnp.clip(1.0 + 0.18 * jax.random.normal(splits[6], (D,), jnp.float32), 0.099609375, 1.8984375).astype(jnp.bfloat16)
    gate_codes = draw_gate_codes(jax.random.fold_in(splits[16], 71), part)
    gate_scale = jnp.clip(jnp.exp(math.log(0.0043945312) - 1.3862944 * jax.random.uniform(splits[8], (D // GROUP, FF), jnp.float32) ** level_of(splits[8], (D // GROUP, FF), ((1, 16),), -0.2, 0.2)), 0.0010986328, 0.0043945312).astype(jnp.bfloat16)
    gate_zero = jnp.clip(6.0 + 3.0 * jax.random.uniform(splits[9], (D // GROUP, FF), jnp.float32) ** level_of(splits[9], (D // GROUP, FF), ((1, 16),), -0.2, 0.2), 6.0, 9.0).astype(jnp.bfloat16)
    up_codes = draw_up_codes(jax.random.fold_in(splits[16], 71), part)
    up_scale = jnp.clip(jnp.exp(math.log(0.0043945312) - 1.3862944 * jax.random.uniform(splits[11], (D // GROUP, FF), jnp.float32) ** level_of(splits[11], (D // GROUP, FF), ((1, 16),), -0.2, 0.2)), 0.0010986328, 0.0043945312).astype(jnp.bfloat16)
    up_zero = jnp.clip(6.0 + 3.0 * jax.random.uniform(splits[12], (D // GROUP, FF), jnp.float32) ** level_of(splits[12], (D // GROUP, FF), ((1, 16),), -0.2, 0.2), 6.0, 9.0).astype(jnp.bfloat16)
    down_codes = draw_down_codes(jax.random.fold_in(splits[16], 71), part)
    down_scale = jnp.clip(jnp.exp(math.log(0.0021972656) - 1.3862944 * jax.random.uniform(splits[14], (FF // GROUP, D), jnp.float32) ** level_of(splits[14], (FF // GROUP, D), ((0, 16),), -0.2, 0.2)), 0.0005493164, 0.0021972656).astype(jnp.bfloat16)
    down_zero = jnp.clip(6.0 + 3.0 * jax.random.uniform(splits[15], (FF // GROUP, D), jnp.float32) ** level_of(splits[15], (FF // GROUP, D), ((0, 16),), -0.2, 0.2), 6.0, 9.0).astype(jnp.bfloat16)
    return dict(residual=residual, query=query, latest_key_value=latest_key_value, kv_cache=kv_cache, lengths=lengths, owner_map=owner_map, norm_gain=norm_gain, gate_codes=gate_codes, gate_scale=gate_scale, gate_zero=gate_zero, up_codes=up_codes, up_scale=up_scale, up_zero=up_zero, down_codes=down_codes, down_scale=down_scale, down_zero=down_zero)


def unpack(packed, zero_point, step_size):
    pieces = []
    for word_slot in range(3):
        digits = 6 if word_slot < 2 else 4
        word = packed[:, word_slot, :]
        for place in range(digits):
            lower = jnp.floor(word / 16.0 ** place)
            upper = jnp.floor(word / 16.0 ** (place + 1))
            pieces.append(lower - 16.0 * upper)
    nibbles = jnp.stack(pieces, axis=1).astype(jnp.float32)
    row_count = packed.shape[0] * 16
    groups = zero_point.shape[0]
    nibbles = nibbles.reshape(groups, row_count // groups, packed.shape[2])
    dequant = (nibbles - zero_point.astype(jnp.float32)[:, None, :]) * step_size.astype(jnp.float32)[:, None, :]
    return dequant.reshape(row_count, packed.shape[2]).astype(jnp.bfloat16)

def attend(single_query, latest_row, cache_block, length):
    key_value_width = KEY_VALUE_HEADS * HEAD_SIZE
    group_width = QUERY_HEADS // KEY_VALUE_HEADS
    inv_root = HEAD_SIZE ** (-0.5)
    query_rows = single_query.astype(jnp.float32).reshape(KEY_VALUE_HEADS, group_width, HEAD_SIZE)
    cached_key_rows = cache_block[:, :key_value_width].astype(jnp.float32).reshape(CONTEXT_TOKENS, KEY_VALUE_HEADS, HEAD_SIZE)
    cached_value_rows = cache_block[:, key_value_width:].astype(jnp.float32).reshape(CONTEXT_TOKENS, KEY_VALUE_HEADS, HEAD_SIZE)
    latest_key = latest_row[:key_value_width].astype(jnp.float32).reshape(KEY_VALUE_HEADS, HEAD_SIZE)
    latest_value = latest_row[key_value_width:].astype(jnp.float32).reshape(KEY_VALUE_HEADS, HEAD_SIZE)
    scores = jnp.einsum('ghd,tgd->ght', query_rows, cached_key_rows) * inv_root
    own_score = jnp.einsum('ghd,gd->gh', query_rows, latest_key) * inv_root
    in_cache = (jnp.arange(CONTEXT_TOKENS, dtype=jnp.int32) < length)[None, None, :]
    largest = jnp.maximum(lax.optimization_barrier(jnp.max(jnp.where(in_cache, scores, -1e+30), axis=-1)), own_score)
    raised = jnp.where(in_cache, jnp.exp(scores - largest[..., None]), 0.0)
    own_raised = jnp.exp(own_score - largest)
    denominator = lax.optimization_barrier(jnp.sum(raised, axis=-1)) + own_raised
    weights = lax.optimization_barrier((raised / denominator[..., None]).astype(jnp.bfloat16))
    own_weight = lax.optimization_barrier((own_raised / denominator).astype(jnp.bfloat16))
    attended = jnp.einsum('ght,tgd->ghd', weights.astype(jnp.float32), cached_value_rows)
    attended = attended + own_weight.astype(jnp.float32)[..., None] * latest_value[:, None, :]
    return attended.reshape(QUERY_HEADS * HEAD_SIZE).astype(jnp.bfloat16)

def reference(residual, query, latest_key_value, kv_cache, lengths, owner_map, norm_gain, gate_codes, gate_scale, gate_zero, up_codes, up_scale, up_zero, down_codes, down_scale, down_zero):

    def one_row(inputs):
        single_query, latest_row, slot = inputs
        return attend(single_query, latest_row, kv_cache[slot], lengths[slot])
    attended = lax.map(one_row, (query, latest_key_value, owner_map))
    stream = (residual.astype(jnp.float32) + attended.astype(jnp.float32)).astype(jnp.bfloat16)
    stream_f = stream.astype(jnp.float32)
    mean_square = lax.optimization_barrier(jnp.mean(stream_f * stream_f, axis=-1, keepdims=True))
    normed = (stream_f * lax.rsqrt(mean_square + 1e-05) * norm_gain.astype(jnp.float32)).astype(jnp.bfloat16)
    block_cols = FF // N_DEV

    def accumulate(block_index, running):
        first = (block_index * block_cols).astype(jnp.int32)
        word_first = (block_index * (block_cols // 16)).astype(jnp.int32)
        group_first = (block_index * (block_cols // GROUP)).astype(jnp.int32)
        w_gate = unpack(lax.dynamic_slice_in_dim(gate_codes, first, block_cols, 2), lax.dynamic_slice_in_dim(gate_zero, first, block_cols, 1), lax.dynamic_slice_in_dim(gate_scale, first, block_cols, 1))
        w_up = unpack(lax.dynamic_slice_in_dim(up_codes, first, block_cols, 2), lax.dynamic_slice_in_dim(up_zero, first, block_cols, 1), lax.dynamic_slice_in_dim(up_scale, first, block_cols, 1))
        w_down = unpack(lax.dynamic_slice_in_dim(down_codes, word_first, block_cols // 16, 0), lax.dynamic_slice_in_dim(down_zero, group_first, block_cols // GROUP, 0), lax.dynamic_slice_in_dim(down_scale, group_first, block_cols // GROUP, 0))
        gate = jnp.dot(normed, w_gate, preferred_element_type=jnp.float32)
        upward = jnp.dot(normed, w_up, preferred_element_type=jnp.float32)
        activated = (jax.nn.silu(gate) * upward).astype(jnp.bfloat16)
        return running + jnp.dot(activated, w_down, preferred_element_type=jnp.float32)
    summed = lax.fori_loop(0, N_DEV, accumulate, jnp.zeros((BATCH_ROWS, D), jnp.float32))
    return (stream_f + summed).astype(jnp.bfloat16)
```

```python
import functools
import jax
import jax.numpy as jnp
from jax import lax
from jax.experimental import pallas as pl
from jax.experimental.pallas import tpu as pltpu
from jax.sharding import PartitionSpec as P

QUERY_HEADS = 64
KEY_VALUE_HEADS = 4
HEAD_SIZE = 128
PLACES = tuple((p, k) for p in range(3) for k in range(6 if p < 2 else 4))


def order_matrix():
    row = lax.broadcasted_iota(jnp.int32, (256, 256), 0)
    col = lax.broadcasted_iota(jnp.int32, (256, 256), 1)
    m = col // 16
    hit = row == (col % 16) * 16 + m
    place = jnp.where(m < 6, m, jnp.where(m < 12, m - 6, m - 12))
    value = jnp.zeros((256, 256), jnp.float32)
    for k in range(6):
        value = jnp.where(place == k, 16.0**-k, value)
    return jnp.where(hit, value, 0.0).astype(jnp.bfloat16)


def unpack_chunk(words_ref, t, scale, zero):
    pieces = []
    zeros = [zero * 16.0**k for k in range(6)]
    for p in range(3):
        word = words_ref[p, pl.ds(t * 16, 16), :].astype(jnp.int32)
        for k in range(6 if p < 2 else 4):
            digit = (word & (15 << (4 * k))).astype(jnp.float32).astype(jnp.bfloat16)
            pieces.append((digit - zeros[k]) * scale)
    return jnp.concatenate(pieces, axis=0)


def rows_of(ref, t, n):
    two = ref[t]
    first = jnp.broadcast_to(two[0:1, :], (8, n))
    second = jnp.broadcast_to(two[1:2, :], (8, n))
    return jnp.concatenate([first, second], axis=0).astype(jnp.bfloat16)


def reorder(x_ref, xp_ref, chunks):
    order = order_matrix()

    def one(t, carry):
        block = x_ref[:, pl.ds(pl.multiple_of(t * 256, 256), 256)]
        xp_ref[t] = jnp.dot(block, order, preferred_element_type=jnp.float32).astype(jnp.bfloat16)
        return carry

    lax.fori_loop(0, chunks, one, 0)


def gate_up_kernel(chunks, x_ref, gc, gs, gz, uc, us, uz, out_ref, xp_ref):
    rows, n = out_ref.shape

    @pl.when(pl.program_id(0) == 0)
    def _():
        reorder(x_ref, xp_ref, chunks)

    def step(t, sums):
        x = xp_ref[t]
        new = []
        for total, c, s, z in zip(sums, (gc, uc), (gs, us), (gz, uz)):
            w = unpack_chunk(c, t, rows_of(s, t, n), rows_of(z, t, n))
            new.append(total + jnp.dot(x, w, preferred_element_type=jnp.float32))
        return tuple(new)

    start = jnp.zeros((rows, n), jnp.float32)
    gate, up = lax.fori_loop(0, chunks, step, (start, start))
    out_ref[...] = (gate / (1.0 + jnp.exp(-gate)) * up).astype(jnp.bfloat16)


def down_kernel(chunks, x_ref, c, s, z, out_ref, xp_ref):
    rows, n = out_ref.shape

    @pl.when(pl.program_id(0) == 0)
    def _():
        reorder(x_ref, xp_ref, chunks)

    def step(t, total):
        w = unpack_chunk(c, t, rows_of(s, t, n), rows_of(z, t, n))
        return total + jnp.dot(xp_ref[t], w, preferred_element_type=jnp.float32)

    out_ref[...] = lax.fori_loop(0, chunks, step, jnp.zeros((rows, n), jnp.float32))


def words_spec(words, n):
    return pl.BlockSpec((3, words, n), lambda j: (0, 0, j))


def pairs_spec(pairs, n):
    return pl.BlockSpec((pairs, 2, n), lambda j: (0, 0, j))


def gate_up(x, gate, up, n):
    rows, depth = x.shape
    width = gate[0].shape[2]
    n = min(n, width)
    chunks = depth // 256
    args = [x]
    specs = [pl.BlockSpec((rows, depth), lambda j: (0, 0))]
    for codes, scale, zero in (gate, up):
        args += [codes.transpose(1, 0, 2)]
        args += [v.astype(jnp.float32).reshape(chunks, 2, width) for v in (scale, zero)]
        specs += [words_spec(depth // 16, n), pairs_spec(chunks, n), pairs_spec(chunks, n)]
    return pl.pallas_call(
        functools.partial(gate_up_kernel, chunks),
        grid=(width // n,),
        out_shape=jax.ShapeDtypeStruct((rows, width), jnp.bfloat16),
        in_specs=specs,
        out_specs=pl.BlockSpec((rows, n), lambda j: (0, j)),
        scratch_shapes=[pltpu.VMEM((chunks, rows, 256), jnp.bfloat16)],
        compiler_params=pltpu.CompilerParams(vmem_limit_bytes=48 << 20),
        name="gate_up",
    )(*args)


def down(x, codes, scale, zero, n):
    rows, depth = x.shape
    width = codes.shape[2]
    chunks = depth // 256
    return pl.pallas_call(
        functools.partial(down_kernel, chunks),
        grid=(width // n,),
        out_shape=jax.ShapeDtypeStruct((rows, width), jnp.float32),
        in_specs=[
            pl.BlockSpec((rows, depth), lambda j: (0, 0)),
            words_spec(depth // 16, n),
            pairs_spec(chunks, n),
            pairs_spec(chunks, n),
        ],
        out_specs=pl.BlockSpec((rows, n), lambda j: (0, j)),
        scratch_shapes=[pltpu.VMEM((chunks, rows, 256), jnp.bfloat16)],
        compiler_params=pltpu.CompilerParams(vmem_limit_bytes=48 << 20),
        name="down",
    )(
        x,
        codes.transpose(1, 0, 2),
        *[v.astype(jnp.float32).reshape(chunks, 2, width) for v in (scale, zero)],
    )


def attend_slots(query_rows, incoming_rows, cache_block, lengths):
    count_of_slots = query_rows.shape[0]
    context_span = cache_block.shape[1]
    key_value_width = KEY_VALUE_HEADS * HEAD_SIZE
    group_width = QUERY_HEADS // KEY_VALUE_HEADS
    inv_root = HEAD_SIZE ** (-0.5)
    grouped_heads = query_rows.reshape(count_of_slots, KEY_VALUE_HEADS, group_width, HEAD_SIZE)
    cached_key_rows = cache_block[:, :, :key_value_width].reshape(
        count_of_slots, context_span, KEY_VALUE_HEADS, HEAD_SIZE
    )
    cached_value_rows = cache_block[:, :, key_value_width:].reshape(
        count_of_slots, context_span, KEY_VALUE_HEADS, HEAD_SIZE
    )
    latest_keys = incoming_rows[:, :key_value_width].reshape(
        count_of_slots, KEY_VALUE_HEADS, HEAD_SIZE
    )
    latest_values = incoming_rows[:, key_value_width:].reshape(
        count_of_slots, KEY_VALUE_HEADS, HEAD_SIZE
    )
    scores = (
        jnp.einsum(
            "sghd,stgd->sght", grouped_heads, cached_key_rows, preferred_element_type=jnp.float32
        )
        * inv_root
    )
    own_score = (
        jnp.einsum("sghd,sgd->sgh", grouped_heads, latest_keys, preferred_element_type=jnp.float32)
        * inv_root
    )
    in_cache = (jnp.arange(context_span, dtype=jnp.int32)[None, :] < lengths[:, None])[
        :, None, None, :
    ]
    largest = jnp.maximum(jnp.max(jnp.where(in_cache, scores, -1e30), axis=-1), own_score)
    raised = jnp.where(in_cache, jnp.exp(scores - largest[..., None]), 0.0)
    own_raised = jnp.exp(own_score - largest)
    denominator = jnp.sum(raised, axis=-1) + own_raised
    weights = (raised / denominator[..., None]).astype(jnp.bfloat16)
    own_weight = (own_raised / denominator).astype(jnp.bfloat16)
    attended = jnp.einsum(
        "sght,stgd->sghd", weights, cached_value_rows, preferred_element_type=jnp.float32
    )
    attended = (
        attended
        + own_weight.astype(jnp.float32)[..., None]
        * latest_values.astype(jnp.float32)[:, :, None, :]
    )
    return attended.reshape(count_of_slots, QUERY_HEADS * HEAD_SIZE).astype(jnp.bfloat16)


def local(
    residual,
    query,
    latest_key_value,
    kv_cache,
    lengths,
    owner_map,
    norm_gain,
    gate_codes,
    gate_scale,
    gate_zero,
    up_codes,
    up_scale,
    up_zero,
    down_codes,
    down_scale,
    down_zero,
):
    own_index = lax.axis_index("dev")
    count_of_slots = kv_cache.shape[0]
    slot_ids = own_index * count_of_slots + jnp.arange(count_of_slots, dtype=jnp.int32)
    chooser = (owner_map[None, :] == slot_ids[:, None]).astype(jnp.bfloat16)

    def select_slots(gathered):
        return jnp.dot(chooser, gathered, preferred_element_type=jnp.float32).astype(jnp.bfloat16)

    every_query, every_new, every_stream = (
        lax.all_gather(query, "dev", axis=0, tiled=True),
        lax.all_gather(latest_key_value, "dev", axis=0, tiled=True),
        lax.all_gather(residual, "dev", axis=0, tiled=True),
    )
    stream_slots = select_slots(every_stream)
    attended = attend_slots(select_slots(every_query), select_slots(every_new), kv_cache, lengths)
    gain_f = norm_gain.astype(jnp.float32)
    slot_stream = (stream_slots.astype(jnp.float32) + attended.astype(jnp.float32)).astype(
        jnp.bfloat16
    )
    every_slot = lax.all_gather(slot_stream, "dev", axis=0, tiled=True)
    stream_all = jnp.take(every_slot, owner_map, axis=0)
    stream_f = stream_all.astype(jnp.float32)
    mean_square = jnp.mean(stream_f * stream_f, axis=-1, keepdims=True)
    normed = (stream_f * lax.rsqrt(mean_square + 1e-05) * gain_f).astype(jnp.bfloat16)
    activated = gate_up(
        normed, (gate_codes, gate_scale, gate_zero), (up_codes, up_scale, up_zero), 256
    )
    products = down(activated, down_codes, down_scale, down_zero, 512)
    row_dev = residual.shape[0]
    own_rows = lax.dynamic_slice_in_dim(stream_all, own_index * row_dev, row_dev, 0)
    summed = lax.psum_scatter(products, "dev", scatter_dimension=0, tiled=True)
    return (own_rows.astype(jnp.float32) + summed).astype(jnp.bfloat16)


def solution(mesh):
    placed = (
        P(("grp", "dev"), None),
        P(("grp", "dev"), None),
        P(("grp", "dev"), None),
        P(("grp", "dev"), None, None),
        P(("grp", "dev")),
        P("grp"),
        P(),
        P(None, None, "dev"),
        P(None, "dev"),
        P(None, "dev"),
        P(None, None, "dev"),
        P(None, "dev"),
        P(None, "dev"),
        P("dev", None, None),
        P("dev", None),
        P("dev", None),
    )
    return jax.shard_map(
        local, mesh=mesh, in_specs=placed, out_specs=P(("grp", "dev"), None), check_vma=False
    )
```

```python
import functools
import jax
import jax.numpy as jnp
from jax import lax
from jax.experimental import pallas as pl
from jax.experimental.pallas import tpu as pltpu
from jax.sharding import PartitionSpec as P

QUERY_HEADS = 64
KEY_VALUE_HEADS = 4
HEAD_SIZE = 128
PLACES = tuple((p, k) for p in range(3) for k in range(6 if p < 2 else 4))


def order_matrix():
    row = lax.broadcasted_iota(jnp.int32, (256, 256), 0)
    col = lax.broadcasted_iota(jnp.int32, (256, 256), 1)
    m = col // 16
    hit = row == (col % 16) * 16 + m
    place = jnp.where(m < 6, m, jnp.where(m < 12, m - 6, m - 12))
    value = jnp.zeros((256, 256), jnp.float32)
    for k in range(6):
        value = jnp.where(place == k, 16.0**-k, value)
    return jnp.where(hit, value, 0.0).astype(jnp.bfloat16)


def unpack_chunk(words_ref, t, scale, zero):
    pieces = []
    zeros = [zero * 16.0**k for k in range(6)]
    for p in range(3):
        word = words_ref[p, pl.ds(t * 16, 16), :].astype(jnp.int32)
        for k in range(6 if p < 2 else 4):
            digit = (word & (15 << (4 * k))).astype(jnp.float32).astype(jnp.bfloat16)
            pieces.append((digit - zeros[k]) * scale)
    return jnp.concatenate(pieces, axis=0)


def rows_of(ref, t, n):
    first = jnp.broadcast_to(ref[pl.ds(2 * t, 1), :], (8, n))
    second = jnp.broadcast_to(ref[pl.ds(2 * t + 1, 1), :], (8, n))
    return jnp.concatenate([first, second], axis=0).astype(jnp.bfloat16)


def reorder(x_ref, xp_ref, chunks):
    order = order_matrix()

    def one(t, carry):
        block = x_ref[:, pl.ds(pl.multiple_of(t * 256, 256), 256)]
        xp_ref[t] = jnp.dot(block, order, preferred_element_type=jnp.float32).astype(jnp.bfloat16)
        return carry

    lax.fori_loop(0, chunks, one, 0)


def widen(sources, targets):
    for source, target in zip(sources, targets):
        target[...] = source[...].astype(jnp.float32)


def gate_up_kernel(chunks, x_ref, gc, gs_in, gz_in, uc, us_in, uz_in, out_ref, xp_ref, gs, gz, us, uz):
    rows, n = out_ref.shape
    widen((gs_in, gz_in, us_in, uz_in), (gs, gz, us, uz))

    @pl.when(pl.program_id(0) == 0)
    def _():
        reorder(x_ref, xp_ref, chunks)

    def step(t, sums):
        x = xp_ref[t]
        new = []
        for total, c, s, z in zip(sums, (gc, uc), (gs, us), (gz, uz)):
            w = unpack_chunk(c, t, rows_of(s, t, n), rows_of(z, t, n))
            new.append(total + jnp.dot(x, w, preferred_element_type=jnp.float32))
        return tuple(new)

    start = jnp.zeros((rows, n), jnp.float32)
    gate, up = lax.fori_loop(0, chunks, step, (start, start))
    out_ref[...] = (gate / (1.0 + jnp.exp(-gate)) * up).astype(jnp.bfloat16)


def down_kernel(chunks, x_ref, c, s_in, z_in, out_ref, xp_ref, s, z):
    rows, n = out_ref.shape
    widen((s_in, z_in), (s, z))

    @pl.when(pl.program_id(0) == 0)
    def _():
        reorder(x_ref, xp_ref, chunks)

    def step(t, total):
        w = unpack_chunk(c, t, rows_of(s, t, n), rows_of(z, t, n))
        return total + jnp.dot(xp_ref[t], w, preferred_element_type=jnp.float32)

    total = lax.fori_loop(0, chunks, step, jnp.zeros((rows, n), jnp.float32))
    out_ref[...] = total.astype(jnp.bfloat16)


def words_spec(words, n):
    return pl.BlockSpec((3, words, n), lambda j: (0, 0, j))


def pairs_spec(pairs, n):
    return pl.BlockSpec((2 * pairs, n), lambda j: (0, j))


def gate_up(x, gate, up, n):
    rows, depth = x.shape
    width = gate[0].shape[2]
    n = min(n, width)
    chunks = depth // 256
    args = [x]
    specs = [pl.BlockSpec((rows, depth), lambda j: (0, 0))]
    for codes, scale, zero in (gate, up):
        args += [codes.transpose(1, 0, 2)]
        args += [scale, zero]
        specs += [words_spec(depth // 16, n), pairs_spec(chunks, n), pairs_spec(chunks, n)]
    return pl.pallas_call(
        functools.partial(gate_up_kernel, chunks),
        grid=(width // n,),
        out_shape=jax.ShapeDtypeStruct((rows, width), jnp.bfloat16),
        in_specs=specs,
        out_specs=pl.BlockSpec((rows, n), lambda j: (0, j)),
        scratch_shapes=[pltpu.VMEM((chunks, rows, 256), jnp.bfloat16)]
        + [pltpu.VMEM((2 * chunks, n), jnp.float32)] * 4,
        compiler_params=pltpu.CompilerParams(vmem_limit_bytes=48 << 20),
        name="gate_up",
    )(*args)


def down(x, codes, scale, zero, n):
    rows, depth = x.shape
    width = codes.shape[2]
    chunks = depth // 256
    return pl.pallas_call(
        functools.partial(down_kernel, chunks),
        grid=(width // n,),
        out_shape=jax.ShapeDtypeStruct((rows, width), jnp.bfloat16),
        in_specs=[
            pl.BlockSpec((rows, depth), lambda j: (0, 0)),
            words_spec(depth // 16, n),
            pairs_spec(chunks, n),
            pairs_spec(chunks, n),
        ],
        out_specs=pl.BlockSpec((rows, n), lambda j: (0, j)),
        scratch_shapes=[pltpu.VMEM((chunks, rows, 256), jnp.bfloat16)]
        + [pltpu.VMEM((2 * chunks, n), jnp.float32)] * 2,
        compiler_params=pltpu.CompilerParams(vmem_limit_bytes=48 << 20),
        name="down",
    )(
        x,
        codes.transpose(1, 0, 2),
        scale,
        zero,
    )


def greet(partners):
    barrier = pltpu.get_barrier_semaphore()
    for partner in partners:
        pl.semaphore_signal(
            barrier, inc=1, device_id={"dev": partner}, device_id_type=pl.DeviceIdType.MESH
        )
    pl.semaphore_wait(barrier, len(partners))


def gather_kernel(outer, x_ref, out_ref, z_send, z_recv, y_send, y_recv, c_send, c_recv, own_sem):
    me = lax.axis_index("dev")
    a, y, c = me // 4, (me // 2) % 2, me % 2
    beside, other = a * 4 + (1 - y) * 2 + c, a * 4 + y * 2 + 1 - c

    def far(d):
        return lax.rem(a + d, outer)

    def push(src, dst, send, recv, to):
        copy = pltpu.make_async_remote_copy(
            src_ref=src,
            dst_ref=dst,
            send_sem=send,
            recv_sem=recv,
            device_id={"dev": to},
            device_id_type=pl.DeviceIdType.MESH,
        )
        copy.start()
        return copy

    greet([far(d) * 4 + y * 2 + c for d in range(1, outer)] + [beside, other])
    own = pltpu.make_async_copy(x_ref, out_ref.at[a, y, c], own_sem)
    own.start()
    here = out_ref.at[a, y, c]
    along = [
        push(x_ref, here, z_send.at[d], z_recv.at[d], far(d) * 4 + y * 2 + c)
        for d in range(1, outer)
    ]
    sides = [push(x_ref, here, y_send.at[0], y_recv.at[0], beside)]
    cores = [push(x_ref, here, c_send.at[0], c_recv.at[0], other)]
    for d in range(1, outer):
        along[d - 1].wait_recv()
        block = out_ref.at[far(outer - d), y, c]
        sides.append(push(block, block, y_send.at[d], y_recv.at[d], beside))
        cores.append(push(block, block, c_send.at[d], c_recv.at[d], other))
    for d in range(outer):
        sides[d].wait_recv()
        block = out_ref.at[far((outer - d) % outer), 1 - y, c]
        cores.append(push(block, block, c_send.at[outer + d], c_recv.at[outer + d], other))
    for copy in cores:
        copy.wait_recv()
    for copy in along + sides + cores:
        copy.wait_send()
    own.wait()


def gather(x, count, number):
    outer = count // 4
    dma = pltpu.SemaphoreType.DMA
    out = pl.pallas_call(
        functools.partial(gather_kernel, outer),
        out_shape=jax.ShapeDtypeStruct((outer, 2, 2) + x.shape, x.dtype),
        in_specs=[pl.BlockSpec(memory_space=pltpu.VMEM)],
        out_specs=pl.BlockSpec(memory_space=pltpu.VMEM),
        scratch_shapes=[dma((outer,))] * 4 + [dma((2 * outer,))] * 2 + [dma],
        compiler_params=pltpu.CompilerParams(
            collective_id=number, has_side_effects=True, vmem_limit_bytes=48 << 20
        ),
        name="gather_%d" % number,
    )(x)
    return out.reshape((count,) + x.shape)


def scatter_kernel(count, x_ref, own_ref, out_ref, got, send, recv):
    me = lax.axis_index("dev")
    to = [lax.rem(me + d, count) for d in range(count)]
    greet(to[1:])
    copies = []
    for d in range(1, count):
        copy = pltpu.make_async_remote_copy(
            src_ref=x_ref.at[to[d]],
            dst_ref=got.at[d],
            send_sem=send.at[d],
            recv_sem=recv.at[d],
            device_id={"dev": to[d]},
            device_id_type=pl.DeviceIdType.MESH,
        )
        copy.start()
        copies.append(copy)
    total = own_ref[...].astype(jnp.float32) + x_ref[me].astype(jnp.float32)
    for d in range(1, count):
        copies[d - 1].wait_recv()
        total = total + got[d].astype(jnp.float32)
    out_ref[...] = total.astype(out_ref.dtype)
    for copy in copies:
        copy.wait_send()


def scatter_sum(x, own, number):
    count = x.shape[0]
    dma = pltpu.SemaphoreType.DMA
    vmem = pl.BlockSpec(memory_space=pltpu.VMEM)
    return pl.pallas_call(
        functools.partial(scatter_kernel, count),
        out_shape=jax.ShapeDtypeStruct(own.shape, own.dtype),
        in_specs=[vmem, vmem],
        out_specs=vmem,
        scratch_shapes=[pltpu.VMEM(x.shape, x.dtype), dma((count,)), dma((count,))],
        compiler_params=pltpu.CompilerParams(
            collective_id=number, has_side_effects=True, vmem_limit_bytes=48 << 20
        ),
        name="scatter_%d" % number,
    )(x, own)


def attend_slots(query_rows, incoming_rows, cache_block, lengths):
    count_of_slots = query_rows.shape[0]
    context_span = cache_block.shape[1]
    key_value_width = KEY_VALUE_HEADS * HEAD_SIZE
    group_width = QUERY_HEADS // KEY_VALUE_HEADS
    inv_root = HEAD_SIZE ** (-0.5)
    grouped_heads = query_rows.reshape(count_of_slots, KEY_VALUE_HEADS, group_width, HEAD_SIZE)
    cached_key_rows = cache_block[:, :, :key_value_width].reshape(
        count_of_slots, context_span, KEY_VALUE_HEADS, HEAD_SIZE
    )
    cached_value_rows = cache_block[:, :, key_value_width:].reshape(
        count_of_slots, context_span, KEY_VALUE_HEADS, HEAD_SIZE
    )
    latest_keys = incoming_rows[:, :key_value_width].reshape(
        count_of_slots, KEY_VALUE_HEADS, HEAD_SIZE
    )
    latest_values = incoming_rows[:, key_value_width:].reshape(
        count_of_slots, KEY_VALUE_HEADS, HEAD_SIZE
    )
    scores = (
        jnp.einsum(
            "sghd,stgd->sght", grouped_heads, cached_key_rows, preferred_element_type=jnp.float32
        )
        * inv_root
    )
    own_score = (
        jnp.einsum("sghd,sgd->sgh", grouped_heads, latest_keys, preferred_element_type=jnp.float32)
        * inv_root
    )
    in_cache = (jnp.arange(context_span, dtype=jnp.int32)[None, :] < lengths[:, None])[
        :, None, None, :
    ]
    largest = jnp.maximum(jnp.max(jnp.where(in_cache, scores, -1e30), axis=-1), own_score)
    raised = jnp.where(in_cache, jnp.exp(scores - largest[..., None]), 0.0)
    own_raised = jnp.exp(own_score - largest)
    denominator = jnp.sum(raised, axis=-1) + own_raised
    weights = (raised / denominator[..., None]).astype(jnp.bfloat16)
    own_weight = (own_raised / denominator).astype(jnp.bfloat16)
    attended = jnp.einsum(
        "sght,stgd->sghd", weights, cached_value_rows, preferred_element_type=jnp.float32
    )
    attended = (
        attended
        + own_weight.astype(jnp.float32)[..., None]
        * latest_values.astype(jnp.float32)[:, :, None, :]
    )
    return attended.reshape(count_of_slots, QUERY_HEADS * HEAD_SIZE).astype(jnp.bfloat16)


def local(
    residual,
    query,
    latest_key_value,
    kv_cache,
    lengths,
    owner_map,
    norm_gain,
    gate_codes,
    gate_scale,
    gate_zero,
    up_codes,
    up_scale,
    up_zero,
    down_codes,
    down_scale,
    down_zero,
):
    own_index = lax.axis_index("dev")
    count_of_slots = kv_cache.shape[0]
    slot_ids = own_index * count_of_slots + jnp.arange(count_of_slots, dtype=jnp.int32)
    chooser = (owner_map[None, :] == slot_ids[:, None]).astype(jnp.bfloat16)

    def select_slots(gathered):
        return jnp.dot(chooser, gathered, preferred_element_type=jnp.float32).astype(jnp.bfloat16)

    count = lax.axis_size("dev")
    row_dev, features = residual.shape
    mine = jnp.concatenate([query, residual, latest_key_value], axis=1)
    every = gather(mine.reshape(16, -1), count, 0).reshape(count * row_dev, -1)
    every_query, every_stream, every_new = (
        every[:, :features],
        every[:, features : 2 * features],
        every[:, 2 * features :],
    )
    stream_slots = select_slots(every_stream)
    attended = attend_slots(select_slots(every_query), select_slots(every_new), kv_cache, lengths)
    gain_f = norm_gain.astype(jnp.float32)
    slot_stream = (stream_slots.astype(jnp.float32) + attended.astype(jnp.float32)).astype(
        jnp.bfloat16
    )
    every_slot = gather(slot_stream.reshape(16, -1), count, 1).reshape(-1, features)
    all_ids = jnp.arange(every_slot.shape[0], dtype=jnp.int32)
    taker = (owner_map[:, None] == all_ids[None, :]).astype(jnp.bfloat16)
    stream_all = jnp.dot(taker, every_slot, preferred_element_type=jnp.float32).astype(jnp.bfloat16)
    stream_f = stream_all.astype(jnp.float32)
    mean_square = jnp.mean(stream_f * stream_f, axis=-1, keepdims=True)
    normed = (stream_f * lax.rsqrt(mean_square + 1e-05) * gain_f).astype(jnp.bfloat16)
    activated = gate_up(
        normed, (gate_codes, gate_scale, gate_zero), (up_codes, up_scale, up_zero), 512
    )
    products = down(activated, down_codes, down_scale, down_zero, 1024)
    own_rows = lax.dynamic_slice_in_dim(stream_all, own_index * row_dev, row_dev, 0)
    return scatter_sum(
        products.reshape(count, 16, -1), own_rows.reshape(16, -1), 2
    ).reshape(row_dev, features)


def solution(mesh):
    placed = (
        P(("grp", "dev"), None),
        P(("grp", "dev"), None),
        P(("grp", "dev"), None),
        P(("grp", "dev"), None, None),
        P(("grp", "dev")),
        P("grp"),
        P(),
        P(None, None, "dev"),
        P(None, "dev"),
        P(None, "dev"),
        P(None, None, "dev"),
        P(None, "dev"),
        P(None, "dev"),
        P("dev", None, None),
        P("dev", None),
        P("dev", None),
    )
    return jax.shard_map(
        local, mesh=mesh, in_specs=placed, out_specs=P(("grp", "dev"), None), check_vma=False
    )
```

```python
import functools
import jax
import jax.numpy as jnp
from jax import lax
from jax.experimental import pallas as pl
from jax.experimental.pallas import tpu as pltpu
from jax.sharding import PartitionSpec as P

QUERY_HEADS = 64
KEY_VALUE_HEADS = 4
HEAD_SIZE = 128
PLACES = tuple((p, k) for p in range(3) for k in range(6 if p < 2 else 4))


def order_matrix():
    row = lax.broadcasted_iota(jnp.int32, (256, 256), 0)
    col = lax.broadcasted_iota(jnp.int32, (256, 256), 1)
    m = col // 16
    hit = row == (col % 16) * 16 + m
    place = jnp.where(m < 6, m, jnp.where(m < 12, m - 6, m - 12))
    value = jnp.zeros((256, 256), jnp.float32)
    for k in range(6):
        value = jnp.where(place == k, 16.0**-k, value)
    return jnp.where(hit, value, 0.0).astype(jnp.bfloat16)


def unpack_chunk(words_ref, t, scale, zero):
    pieces = []
    zeros = [zero * 16.0**k for k in range(6)]
    for p in range(3):
        word = words_ref[p, pl.ds(t * 16, 16), :].astype(jnp.int32)
        for k in range(6 if p < 2 else 4):
            digit = (word & (15 << (4 * k))).astype(jnp.float32).astype(jnp.bfloat16)
            pieces.append((digit - zeros[k]) * scale)
    return jnp.concatenate(pieces, axis=0)


def rows_of(ref, t, n):
    first = jnp.broadcast_to(ref[pl.ds(2 * t, 1), :], (8, n))
    second = jnp.broadcast_to(ref[pl.ds(2 * t + 1, 1), :], (8, n))
    return jnp.concatenate([first, second], axis=0).astype(jnp.bfloat16)


def reorder(x_ref, xp_ref, chunks):
    order = order_matrix()

    def one(t, carry):
        block = x_ref[:, pl.ds(pl.multiple_of(t * 256, 256), 256)]
        xp_ref[t] = jnp.dot(block, order, preferred_element_type=jnp.float32).astype(jnp.bfloat16)
        return carry

    lax.fori_loop(0, chunks, one, 0)


def widen(sources, targets):
    for source, target in zip(sources, targets):
        target[...] = source[...].astype(jnp.float32)


def gate_up_kernel(chunks, x_ref, gc, gs_in, gz_in, uc, us_in, uz_in, out_ref, xp_ref, gs, gz, us, uz):
    rows, n = out_ref.shape
    widen((gs_in, gz_in, us_in, uz_in), (gs, gz, us, uz))

    @pl.when(pl.program_id(0) == 0)
    def _():
        reorder(x_ref, xp_ref, chunks)

    def step(t, sums):
        x = xp_ref[t]
        new = []
        for total, c, s, z in zip(sums, (gc, uc), (gs, us), (gz, uz)):
            w = unpack_chunk(c, t, rows_of(s, t, n), rows_of(z, t, n))
            new.append(total + jnp.dot(x, w, preferred_element_type=jnp.float32))
        return tuple(new)

    start = jnp.zeros((rows, n), jnp.float32)
    gate, up = lax.fori_loop(0, chunks, step, (start, start), unroll=min(8, chunks))
    out_ref[...] = (gate / (1.0 + jnp.exp(-gate)) * up).astype(jnp.bfloat16)


def down_kernel(
    chunks, count, x_ref, c, s_in, z_in, own_ref, out_ref, xp_ref, s, z, mine, got, send, recv
):
    rows, n = x_ref.shape[0], s.shape[1]
    each = rows // count
    j, steps = pl.program_id(0), pl.num_programs(0)
    me = lax.axis_index("dev")
    to = [lax.rem(me + d, count) for d in range(count)]
    widen((s_in, z_in), (s, z))

    def copy(tile, d):
        return pltpu.make_async_remote_copy(
            src_ref=mine.at[tile, to[d]],
            dst_ref=got.at[tile, d],
            send_sem=send.at[tile, d],
            recv_sem=recv.at[tile, d],
            device_id={"dev": to[d]},
            device_id_type=pl.DeviceIdType.MESH,
        )

    @pl.when(j == 0)
    def _():
        greet(to[1:])
        reorder(x_ref, xp_ref, chunks)

    def step(t, total):
        w = unpack_chunk(c, t, rows_of(s, t, n), rows_of(z, t, n))
        return total + jnp.dot(xp_ref[t], w, preferred_element_type=jnp.float32)

    start = jnp.zeros((rows, n), jnp.float32)
    total = lax.fori_loop(0, chunks, step, start, unroll=min(8, chunks))
    total = total.astype(jnp.bfloat16)
    for d in range(count):
        mine[j, d] = total[each * d : each * (d + 1), :]
    for d in range(1, count):
        copy(j, d).start()

    @pl.when(j == steps - 1)
    def _():
        def finish(tile, carry):
            here = pl.ds(pl.multiple_of(tile * n, n), n)
            summed = own_ref[:, here].astype(jnp.float32) + mine[tile, me].astype(jnp.float32)
            for d in range(1, count):
                copy(tile, d).wait_recv()
                summed = summed + got[tile, d].astype(jnp.float32)
            out_ref[:, here] = summed.astype(jnp.bfloat16)
            for d in range(1, count):
                copy(tile, d).wait_send()
            return carry

        lax.fori_loop(0, steps, finish, 0)


def words_spec(words, n):
    return pl.BlockSpec((3, words, n), lambda j: (0, 0, j))


def pairs_spec(pairs, n):
    return pl.BlockSpec((2 * pairs, n), lambda j: (0, j))


def gate_up(x, gate, up, n):
    rows, depth = x.shape
    width = gate[0].shape[2]
    n = min(n, width)
    chunks = depth // 256
    args = [x]
    specs = [pl.BlockSpec((rows, depth), lambda j: (0, 0))]
    for codes, scale, zero in (gate, up):
        args += [codes.transpose(1, 0, 2)]
        args += [scale, zero]
        specs += [words_spec(depth // 16, n), pairs_spec(chunks, n), pairs_spec(chunks, n)]
    return pl.pallas_call(
        functools.partial(gate_up_kernel, chunks),
        grid=(width // n,),
        out_shape=jax.ShapeDtypeStruct((rows, width), jnp.bfloat16),
        in_specs=specs,
        out_specs=pl.BlockSpec((rows, n), lambda j: (0, j)),
        scratch_shapes=[pltpu.VMEM((chunks, rows, 256), jnp.bfloat16)]
        + [pltpu.VMEM((2 * chunks, n), jnp.float32)] * 4,
        compiler_params=pltpu.CompilerParams(vmem_limit_bytes=48 << 20),
        name="gate_up",
    )(*args)


def down(x, codes, scale, zero, own, count, n, number):
    rows, depth = x.shape
    width = codes.shape[2]
    chunks = depth // 256
    steps = width // n
    dma = pltpu.SemaphoreType.DMA
    blocks = pltpu.VMEM((steps, count, rows // count, n), jnp.bfloat16)
    return pl.pallas_call(
        functools.partial(down_kernel, chunks, count),
        grid=(steps,),
        out_shape=jax.ShapeDtypeStruct(own.shape, own.dtype),
        in_specs=[
            pl.BlockSpec((rows, depth), lambda j: (0, 0)),
            words_spec(depth // 16, n),
            pairs_spec(chunks, n),
            pairs_spec(chunks, n),
            pl.BlockSpec(own.shape, lambda j: (0, 0)),
        ],
        out_specs=pl.BlockSpec(own.shape, lambda j: (0, 0)),
        scratch_shapes=[pltpu.VMEM((chunks, rows, 256), jnp.bfloat16)]
        + [pltpu.VMEM((2 * chunks, n), jnp.float32)] * 2
        + [blocks, blocks, dma((steps, count)), dma((steps, count))],
        compiler_params=pltpu.CompilerParams(
            collective_id=number, has_side_effects=True, vmem_limit_bytes=48 << 20
        ),
        name="down",
    )(x, codes.transpose(1, 0, 2), scale, zero, own)


def greet(partners):
    barrier = pltpu.get_barrier_semaphore()
    for partner in partners:
        pl.semaphore_signal(
            barrier, inc=1, device_id={"dev": partner}, device_id_type=pl.DeviceIdType.MESH
        )
    pl.semaphore_wait(barrier, len(partners))


def gather_kernel(outer, x_ref, out_ref, z_send, z_recv, y_send, y_recv, c_send, c_recv, own_sem):
    me = lax.axis_index("dev")
    a, y, c = me // 4, (me // 2) % 2, me % 2
    beside, other = a * 4 + (1 - y) * 2 + c, a * 4 + y * 2 + 1 - c

    def far(d):
        return lax.rem(a + d, outer)

    def push(src, dst, send, recv, to):
        copy = pltpu.make_async_remote_copy(
            src_ref=src,
            dst_ref=dst,
            send_sem=send,
            recv_sem=recv,
            device_id={"dev": to},
            device_id_type=pl.DeviceIdType.MESH,
        )
        copy.start()
        return copy

    greet([far(d) * 4 + y * 2 + c for d in range(1, outer)] + [beside, other])
    own = pltpu.make_async_copy(x_ref, out_ref.at[a, y, c], own_sem)
    own.start()
    here = out_ref.at[a, y, c]
    along = [
        push(x_ref, here, z_send.at[d], z_recv.at[d], far(d) * 4 + y * 2 + c)
        for d in range(1, outer)
    ]
    sides = [push(x_ref, here, y_send.at[0], y_recv.at[0], beside)]
    cores = [push(x_ref, here, c_send.at[0], c_recv.at[0], other)]
    for d in range(1, outer):
        along[d - 1].wait_recv()
        block = out_ref.at[far(outer - d), y, c]
        sides.append(push(block, block, y_send.at[d], y_recv.at[d], beside))
        cores.append(push(block, block, c_send.at[d], c_recv.at[d], other))
    for d in range(outer):
        sides[d].wait_recv()
        block = out_ref.at[far((outer - d) % outer), 1 - y, c]
        cores.append(push(block, block, c_send.at[outer + d], c_recv.at[outer + d], other))
    for copy in cores:
        copy.wait_recv()
    for copy in along + sides + cores:
        copy.wait_send()
    own.wait()


def gather(x, count, number):
    outer = count // 4
    dma = pltpu.SemaphoreType.DMA
    out = pl.pallas_call(
        functools.partial(gather_kernel, outer),
        out_shape=jax.ShapeDtypeStruct((outer, 2, 2) + x.shape, x.dtype),
        in_specs=[pl.BlockSpec(memory_space=pltpu.VMEM)],
        out_specs=pl.BlockSpec(memory_space=pltpu.VMEM),
        scratch_shapes=[dma((outer,))] * 4 + [dma((2 * outer,))] * 2 + [dma],
        compiler_params=pltpu.CompilerParams(
            collective_id=number, has_side_effects=True, vmem_limit_bytes=48 << 20
        ),
        name="gather_%d" % number,
    )(x)
    return out.reshape((count,) + x.shape)


def attend_slots(query_rows, incoming_rows, cache_block, lengths):
    count_of_slots = query_rows.shape[0]
    context_span = cache_block.shape[1]
    key_value_width = KEY_VALUE_HEADS * HEAD_SIZE
    group_width = QUERY_HEADS // KEY_VALUE_HEADS
    inv_root = HEAD_SIZE ** (-0.5)
    grouped_heads = query_rows.reshape(count_of_slots, KEY_VALUE_HEADS, group_width, HEAD_SIZE)
    cached_key_rows = cache_block[:, :, :key_value_width].reshape(
        count_of_slots, context_span, KEY_VALUE_HEADS, HEAD_SIZE
    )
    cached_value_rows = cache_block[:, :, key_value_width:].reshape(
        count_of_slots, context_span, KEY_VALUE_HEADS, HEAD_SIZE
    )
    latest_keys = incoming_rows[:, :key_value_width].reshape(
        count_of_slots, KEY_VALUE_HEADS, HEAD_SIZE
    )
    latest_values = incoming_rows[:, key_value_width:].reshape(
        count_of_slots, KEY_VALUE_HEADS, HEAD_SIZE
    )
    scores = (
        jnp.einsum(
            "sghd,stgd->sght", grouped_heads, cached_key_rows, preferred_element_type=jnp.float32
        )
        * inv_root
    )
    own_score = (
        jnp.einsum("sghd,sgd->sgh", grouped_heads, latest_keys, preferred_element_type=jnp.float32)
        * inv_root
    )
    in_cache = (jnp.arange(context_span, dtype=jnp.int32)[None, :] < lengths[:, None])[
        :, None, None, :
    ]
    largest = jnp.maximum(jnp.max(jnp.where(in_cache, scores, -1e30), axis=-1), own_score)
    raised = jnp.where(in_cache, jnp.exp(scores - largest[..., None]), 0.0)
    own_raised = jnp.exp(own_score - largest)
    denominator = jnp.sum(raised, axis=-1) + own_raised
    weights = (raised / denominator[..., None]).astype(jnp.bfloat16)
    own_weight = (own_raised / denominator).astype(jnp.bfloat16)
    attended = jnp.einsum(
        "sght,stgd->sghd", weights, cached_value_rows, preferred_element_type=jnp.float32
    )
    attended = (
        attended
        + own_weight.astype(jnp.float32)[..., None]
        * latest_values.astype(jnp.float32)[:, :, None, :]
    )
    return attended.reshape(count_of_slots, QUERY_HEADS * HEAD_SIZE).astype(jnp.bfloat16)


def local(
    residual,
    query,
    latest_key_value,
    kv_cache,
    lengths,
    owner_map,
    norm_gain,
    gate_codes,
    gate_scale,
    gate_zero,
    up_codes,
    up_scale,
    up_zero,
    down_codes,
    down_scale,
    down_zero,
):
    own_index = lax.axis_index("dev")
    count_of_slots = kv_cache.shape[0]
    slot_ids = own_index * count_of_slots + jnp.arange(count_of_slots, dtype=jnp.int32)
    chooser = (owner_map[None, :] == slot_ids[:, None]).astype(jnp.bfloat16)

    def select_slots(gathered):
        return jnp.dot(chooser, gathered, preferred_element_type=jnp.float32).astype(jnp.bfloat16)

    count = lax.axis_size("dev")
    row_dev, features = residual.shape
    mine = jnp.concatenate([query, residual, latest_key_value], axis=1)
    every = gather(mine.reshape(16, -1), count, 0).reshape(count * row_dev, -1)
    every_query, every_stream, every_new = (
        every[:, :features],
        every[:, features : 2 * features],
        every[:, 2 * features :],
    )
    stream_slots = select_slots(every_stream)
    attended = attend_slots(select_slots(every_query), select_slots(every_new), kv_cache, lengths)
    gain_f = norm_gain.astype(jnp.float32)
    slot_stream = (stream_slots.astype(jnp.float32) + attended.astype(jnp.float32)).astype(
        jnp.bfloat16
    )
    every_slot = gather(slot_stream.reshape(16, -1), count, 1).reshape(-1, features)
    all_ids = jnp.arange(every_slot.shape[0], dtype=jnp.int32)
    taker = (owner_map[:, None] == all_ids[None, :]).astype(jnp.bfloat16)
    stream_all = jnp.dot(taker, every_slot, preferred_element_type=jnp.float32).astype(jnp.bfloat16)
    stream_f = stream_all.astype(jnp.float32)
    mean_square = jnp.mean(stream_f * stream_f, axis=-1, keepdims=True)
    normed = (stream_f * lax.rsqrt(mean_square + 1e-05) * gain_f).astype(jnp.bfloat16)
    activated = gate_up(
        normed, (gate_codes, gate_scale, gate_zero), (up_codes, up_scale, up_zero), 512
    )
    own_rows = lax.dynamic_slice_in_dim(stream_all, own_index * row_dev, row_dev, 0)
    return down(activated, down_codes, down_scale, down_zero, own_rows, count, 1024, 2)


def solution(mesh):
    placed = (
        P(("grp", "dev"), None),
        P(("grp", "dev"), None),
        P(("grp", "dev"), None),
        P(("grp", "dev"), None, None),
        P(("grp", "dev")),
        P("grp"),
        P(),
        P(None, None, "dev"),
        P(None, "dev"),
        P(None, "dev"),
        P(None, None, "dev"),
        P(None, "dev"),
        P(None, "dev"),
        P("dev", None, None),
        P("dev", None),
        P("dev", None),
    )
    return jax.shard_map(
        local, mesh=mesh, in_specs=placed, out_specs=P(("grp", "dev"), None), check_vma=False
    )
```

```python
import functools
import jax
import jax.numpy as jnp
from jax import lax
from jax.experimental import pallas as pl
from jax.experimental.pallas import tpu as pltpu
from jax.sharding import PartitionSpec as P

QUERY_HEADS = 64
KEY_VALUE_HEADS = 4
HEAD_SIZE = 128
PLACES = tuple((p, k) for p in range(3) for k in range(6 if p < 2 else 4))


def order_matrix():
    row = lax.broadcasted_iota(jnp.int32, (256, 256), 0)
    col = lax.broadcasted_iota(jnp.int32, (256, 256), 1)
    m = col // 16
    hit = row == (col % 16) * 16 + m
    place = jnp.where(m < 6, m, jnp.where(m < 12, m - 6, m - 12))
    value = jnp.zeros((256, 256), jnp.float32)
    for k in range(6):
        value = jnp.where(place == k, 16.0**-k, value)
    return jnp.where(hit, value, 0.0).astype(jnp.bfloat16)


def unpack_chunk(words_ref, t, scale, zero):
    pieces = []
    zeros = [zero * 16.0**k for k in range(6)]
    for p in range(3):
        word = words_ref[p, pl.ds(t * 16, 16), :].astype(jnp.int32)
        for k in range(6 if p < 2 else 4):
            digit = (word & (15 << (4 * k))).astype(jnp.float32).astype(jnp.bfloat16)
            pieces.append((digit - zeros[k]) * scale)
    return jnp.concatenate(pieces, axis=0)


def rows_of(ref, t, n):
    first = jnp.broadcast_to(ref[pl.ds(2 * t, 1), :], (8, n))
    second = jnp.broadcast_to(ref[pl.ds(2 * t + 1, 1), :], (8, n))
    return jnp.concatenate([first, second], axis=0).astype(jnp.bfloat16)


def reorder(x_ref, xp_ref, chunks):
    order = order_matrix()

    def one(t, carry):
        block = x_ref[:, pl.ds(pl.multiple_of(t * 256, 256), 256)]
        xp_ref[t] = jnp.dot(block, order, preferred_element_type=jnp.float32).astype(jnp.bfloat16)
        return carry

    lax.fori_loop(0, chunks, one, 0)


def widen(sources, targets):
    for source, target in zip(sources, targets):
        target[...] = source[...].astype(jnp.float32)


def gate_up_kernel(chunks, x_ref, gc, gs_in, gz_in, uc, us_in, uz_in, out_ref, xp_ref, gs, gz, us, uz):
    rows, n = out_ref.shape
    widen((gs_in, gz_in, us_in, uz_in), (gs, gz, us, uz))

    @pl.when(pl.program_id(0) == 0)
    def _():
        reorder(x_ref, xp_ref, chunks)

    def step(t, sums):
        x = xp_ref[t]
        new = []
        for total, c, s, z in zip(sums, (gc, uc), (gs, us), (gz, uz)):
            w = unpack_chunk(c, t, rows_of(s, t, n), rows_of(z, t, n))
            new.append(total + jnp.dot(x, w, preferred_element_type=jnp.float32))
        return tuple(new)

    start = jnp.zeros((rows, n), jnp.float32)
    gate, up = lax.fori_loop(0, chunks, step, (start, start), unroll=min(8, chunks))
    out_ref[...] = (gate / (1.0 + jnp.exp(-gate)) * up).astype(jnp.bfloat16)


def down_kernel(
    chunks, count, x_ref, c, s_in, z_in, own_ref, out_ref, xp_ref, s, z, mine, got, send, recv
):
    rows, n = x_ref.shape[0], s.shape[1]
    each = rows // count
    j, steps = pl.program_id(0), pl.num_programs(0)
    me = lax.axis_index("dev")
    to = [lax.rem(me + d, count) for d in range(count)]
    widen((s_in, z_in), (s, z))

    def copy(tile, d):
        return pltpu.make_async_remote_copy(
            src_ref=mine.at[tile, to[d]],
            dst_ref=got.at[tile, d],
            send_sem=send.at[tile, d],
            recv_sem=recv.at[tile, d],
            device_id={"dev": to[d]},
            device_id_type=pl.DeviceIdType.MESH,
        )

    @pl.when(j == 0)
    def _():
        greet(to[1:])
        reorder(x_ref, xp_ref, chunks)

    def step(t, total):
        w = unpack_chunk(c, t, rows_of(s, t, n), rows_of(z, t, n))
        return total + jnp.dot(xp_ref[t], w, preferred_element_type=jnp.float32)

    start = jnp.zeros((rows, n), jnp.float32)
    total = lax.fori_loop(0, chunks, step, start, unroll=min(8, chunks))
    total = total.astype(jnp.bfloat16)
    for d in range(count):
        mine[j, d] = total[each * d : each * (d + 1), :]
    for d in range(1, count):
        copy(j, d).start()

    @pl.when(j == steps - 1)
    def _():
        def finish(tile, carry):
            here = pl.ds(pl.multiple_of(tile * n, n), n)
            summed = own_ref[:, here].astype(jnp.float32) + mine[tile, me].astype(jnp.float32)
            for d in range(1, count):
                copy(tile, d).wait_recv()
                summed = summed + got[tile, d].astype(jnp.float32)
            out_ref[:, here] = summed.astype(jnp.bfloat16)
            for d in range(1, count):
                copy(tile, d).wait_send()
            return carry

        lax.fori_loop(0, steps, finish, 0)


def words_spec(words, n):
    return pl.BlockSpec((3, words, n), lambda j: (0, 0, j))


def pairs_spec(pairs, n):
    return pl.BlockSpec((2 * pairs, n), lambda j: (0, j))


def gate_up(x, gate, up, n):
    rows, depth = x.shape
    width = gate[0].shape[2]
    n = min(n, width)
    chunks = depth // 256
    args = [x]
    specs = [pl.BlockSpec((rows, depth), lambda j: (0, 0))]
    for codes, scale, zero in (gate, up):
        args += [codes.transpose(1, 0, 2)]
        args += [scale, zero]
        specs += [words_spec(depth // 16, n), pairs_spec(chunks, n), pairs_spec(chunks, n)]
    return pl.pallas_call(
        functools.partial(gate_up_kernel, chunks),
        grid=(width // n,),
        out_shape=jax.ShapeDtypeStruct((rows, width), jnp.bfloat16),
        in_specs=specs,
        out_specs=pl.BlockSpec((rows, n), lambda j: (0, j)),
        scratch_shapes=[pltpu.VMEM((chunks, rows, 256), jnp.bfloat16)]
        + [pltpu.VMEM((2 * chunks, n), jnp.float32)] * 4,
        compiler_params=pltpu.CompilerParams(vmem_limit_bytes=48 << 20),
        name="gate_up",
    )(*args)


def down(x, codes, scale, zero, own, count, n, number):
    rows, depth = x.shape
    width = codes.shape[2]
    chunks = depth // 256
    steps = width // n
    dma = pltpu.SemaphoreType.DMA
    blocks = pltpu.VMEM((steps, count, rows // count, n), jnp.bfloat16)
    return pl.pallas_call(
        functools.partial(down_kernel, chunks, count),
        grid=(steps,),
        out_shape=jax.ShapeDtypeStruct(own.shape, own.dtype),
        in_specs=[
            pl.BlockSpec((rows, depth), lambda j: (0, 0)),
            words_spec(depth // 16, n),
            pairs_spec(chunks, n),
            pairs_spec(chunks, n),
            pl.BlockSpec(own.shape, lambda j: (0, 0)),
        ],
        out_specs=pl.BlockSpec(own.shape, lambda j: (0, 0)),
        scratch_shapes=[pltpu.VMEM((chunks, rows, 256), jnp.bfloat16)]
        + [pltpu.VMEM((2 * chunks, n), jnp.float32)] * 2
        + [blocks, blocks, dma((steps, count)), dma((steps, count))],
        compiler_params=pltpu.CompilerParams(
            collective_id=number, has_side_effects=True, vmem_limit_bytes=48 << 20
        ),
        name="down",
    )(x, codes.transpose(1, 0, 2), scale, zero, own)


def greet(partners):
    barrier = pltpu.get_barrier_semaphore()
    for partner in partners:
        pl.semaphore_signal(
            barrier, inc=1, device_id={"dev": partner}, device_id_type=pl.DeviceIdType.MESH
        )
    pl.semaphore_wait(barrier, len(partners))


def gather_kernel(outer, x_ref, out_ref, z_send, z_recv, y_send, y_recv, c_send, c_recv, own_sem):
    me = lax.axis_index("dev")
    a, y, c = me // 4, (me // 2) % 2, me % 2
    beside, other = a * 4 + (1 - y) * 2 + c, a * 4 + y * 2 + 1 - c

    def far(d):
        return lax.rem(a + d, outer)

    def push(src, dst, send, recv, to):
        copy = pltpu.make_async_remote_copy(
            src_ref=src,
            dst_ref=dst,
            send_sem=send,
            recv_sem=recv,
            device_id={"dev": to},
            device_id_type=pl.DeviceIdType.MESH,
        )
        copy.start()
        return copy

    greet([far(d) * 4 + y * 2 + c for d in range(1, outer)] + [beside, other])
    own = pltpu.make_async_copy(x_ref, out_ref.at[a, y, c], own_sem)
    own.start()
    here = out_ref.at[a, y, c]
    along = [
        push(x_ref, here, z_send.at[d], z_recv.at[d], far(d) * 4 + y * 2 + c)
        for d in range(1, outer)
    ]
    sides = [push(x_ref, here, y_send.at[0], y_recv.at[0], beside)]
    cores = [push(x_ref, here, c_send.at[0], c_recv.at[0], other)]
    for d in range(1, outer):
        along[d - 1].wait_recv()
        block = out_ref.at[far(outer - d), y, c]
        sides.append(push(block, block, y_send.at[d], y_recv.at[d], beside))
        cores.append(push(block, block, c_send.at[d], c_recv.at[d], other))
    for d in range(outer):
        sides[d].wait_recv()
        block = out_ref.at[far((outer - d) % outer), 1 - y, c]
        cores.append(push(block, block, c_send.at[outer + d], c_recv.at[outer + d], other))
    for copy in cores:
        copy.wait_recv()
    for copy in along + sides + cores:
        copy.wait_send()
    own.wait()


def gather(x, count, number):
    outer = count // 4
    dma = pltpu.SemaphoreType.DMA
    out = pl.pallas_call(
        functools.partial(gather_kernel, outer),
        out_shape=jax.ShapeDtypeStruct((outer, 2, 2) + x.shape, x.dtype),
        in_specs=[pl.BlockSpec(memory_space=pltpu.VMEM)],
        out_specs=pl.BlockSpec(memory_space=pltpu.VMEM),
        scratch_shapes=[dma((outer,))] * 4 + [dma((2 * outer,))] * 2 + [dma],
        compiler_params=pltpu.CompilerParams(
            collective_id=number, has_side_effects=True, vmem_limit_bytes=48 << 20
        ),
        name="gather_%d" % number,
    )(x)
    return out.reshape((count,) + x.shape)


def attend_slots(query_rows, incoming_rows, cache_block, lengths):
    count_of_slots = query_rows.shape[0]
    context_span = cache_block.shape[1]
    key_value_width = KEY_VALUE_HEADS * HEAD_SIZE
    group_width = QUERY_HEADS // KEY_VALUE_HEADS
    inv_root = HEAD_SIZE ** (-0.5)
    grouped_heads = query_rows.reshape(count_of_slots, KEY_VALUE_HEADS, group_width, HEAD_SIZE)
    cached_key_rows = cache_block[:, :, :key_value_width].reshape(
        count_of_slots, context_span, KEY_VALUE_HEADS, HEAD_SIZE
    )
    cached_value_rows = cache_block[:, :, key_value_width:].reshape(
        count_of_slots, context_span, KEY_VALUE_HEADS, HEAD_SIZE
    )
    latest_keys = incoming_rows[:, :key_value_width].reshape(
        count_of_slots, KEY_VALUE_HEADS, HEAD_SIZE
    )
    latest_values = incoming_rows[:, key_value_width:].reshape(
        count_of_slots, KEY_VALUE_HEADS, HEAD_SIZE
    )
    scores = (
        jnp.einsum(
            "sghd,stgd->sght", grouped_heads, cached_key_rows, preferred_element_type=jnp.float32
        )
        * inv_root
    )
    own_score = (
        jnp.einsum("sghd,sgd->sgh", grouped_heads, latest_keys, preferred_element_type=jnp.float32)
        * inv_root
    )
    in_cache = (jnp.arange(context_span, dtype=jnp.int32)[None, :] < lengths[:, None])[
        :, None, None, :
    ]
    largest = jnp.maximum(jnp.max(jnp.where(in_cache, scores, -1e30), axis=-1), own_score)
    raised = jnp.where(in_cache, jnp.exp(scores - largest[..., None]), 0.0)
    own_raised = jnp.exp(own_score - largest)
    denominator = jnp.sum(raised, axis=-1) + own_raised
    weights = (raised / denominator[..., None]).astype(jnp.bfloat16)
    own_weight = (own_raised / denominator).astype(jnp.bfloat16)
    attended = jnp.einsum(
        "sght,stgd->sghd", weights, cached_value_rows, preferred_element_type=jnp.float32
    )
    attended = (
        attended
        + own_weight.astype(jnp.float32)[..., None]
        * latest_values.astype(jnp.float32)[:, :, None, :]
    )
    return attended.reshape(count_of_slots, QUERY_HEADS * HEAD_SIZE).astype(jnp.bfloat16)


def local(
    residual,
    query,
    latest_key_value,
    kv_cache,
    lengths,
    owner_map,
    norm_gain,
    gate_codes,
    gate_scale,
    gate_zero,
    up_codes,
    up_scale,
    up_zero,
    down_codes,
    down_scale,
    down_zero,
):
    own_index = lax.axis_index("dev")
    count_of_slots = kv_cache.shape[0]
    slot_ids = own_index * count_of_slots + jnp.arange(count_of_slots, dtype=jnp.int32)
    chooser = (owner_map[None, :] == slot_ids[:, None]).astype(jnp.bfloat16)

    def select_slots(gathered):
        return jnp.dot(chooser, gathered, preferred_element_type=jnp.float32).astype(jnp.bfloat16)

    count = lax.axis_size("dev")
    row_dev, features = residual.shape
    mine = jnp.concatenate([query, residual, latest_key_value], axis=1)
    every = gather(mine.reshape(16, -1), count, 0).reshape(count * row_dev, -1)
    every_query, every_stream, every_new = (
        every[:, :features],
        every[:, features : 2 * features],
        every[:, 2 * features :],
    )
    stream_slots = select_slots(every_stream)
    attended = attend_slots(select_slots(every_query), select_slots(every_new), kv_cache, lengths)
    gain_f = norm_gain.astype(jnp.float32)
    slot_stream = (stream_slots.astype(jnp.float32) + attended.astype(jnp.float32)).astype(
        jnp.bfloat16
    )
    every_slot = gather(slot_stream.reshape(16, -1), count, 1).reshape(-1, features)
    all_ids = jnp.arange(every_slot.shape[0], dtype=jnp.int32)
    taker = (owner_map[:, None] == all_ids[None, :]).astype(jnp.bfloat16)
    stream_all = jnp.dot(taker, every_slot, preferred_element_type=jnp.float32).astype(jnp.bfloat16)
    stream_f = stream_all.astype(jnp.float32)
    mean_square = jnp.mean(stream_f * stream_f, axis=-1, keepdims=True)
    normed = (stream_f * lax.rsqrt(mean_square + 1e-05) * gain_f).astype(jnp.bfloat16)
    activated = gate_up(
        normed, (gate_codes, gate_scale, gate_zero), (up_codes, up_scale, up_zero), 512
    )
    own_rows = lax.dynamic_slice_in_dim(stream_all, own_index * row_dev, row_dev, 0)
    return down(activated, down_codes, down_scale, down_zero, own_rows, count, 2048, 2)


def solution(mesh):
    placed = (
        P(("grp", "dev"), None),
        P(("grp", "dev"), None),
        P(("grp", "dev"), None),
        P(("grp", "dev"), None, None),
        P(("grp", "dev")),
        P("grp"),
        P(),
        P(None, None, "dev"),
        P(None, "dev"),
        P(None, "dev"),
        P(None, None, "dev"),
        P(None, "dev"),
        P(None, "dev"),
        P("dev", None, None),
        P("dev", None),
        P("dev", None),
    )
    return jax.shard_map(
        local, mesh=mesh, in_specs=placed, out_specs=P(("grp", "dev"), None), check_vma=False
    )
```
